32 devices in a mesh: grp: 2 (over y), seq: 4 (over z), col: 4 (over x, core).
Axes of the slice: x: 2, y: 2, z: 4, core: 2. Of those that a mesh axis runs over, the one named last changes fastest.
Arguments:
- tokens: bfloat16 [4096, 4608], P(('grp', 'seq'), 'col'), parts along dimension 0, may hold values from -14 to 14
- norm_gain: float32 [4608], replicated, may hold values from 0.5 to 1.5
- query_weight: bfloat16 [4608, 2048], P('seq', 'col'), may hold values from -1 to 1
- key_weight: bfloat16 [4608, 1024], P('seq', 'col'), may hold values from -1 to 1
- value_weight: bfloat16 [4608, 1024], P('seq', 'col'), may hold values from -0.09375 to 0.09375
- out_weight: bfloat16 [2048, 4608], P('seq', 'col'), may hold values from -1 to 1
- positions: int32 [4096], P(('grp', 'seq')), parts along dimension 0, may hold values from 0 to 2047, as said below
Outputs:
- block_out: bfloat16 [4096, 4608], P(('grp', 'seq'), 'col'), parts along dimension 0
The draws below stay inside these ranges and needn't reach their ends.
There are 2 independent parts, one for each index of `grp`. The reference program is written for one: setup_inputs(seed, part) draws one part's arguments, and reference() takes and returns one part's arrays. A program takes and returns all parts, laid end to end along the dimension named above; an argument that names none is the same for every part. Nothing has to cross between parts.
Inputs may be any that keep to these rules, and one draw needn't show every extreme that they name: Within a document positions rise by one from token to token. Exactly one document starts inside the slab, at a token of its middle half, where positions restart at 0; the document before it ends at position 2047.
All inputs are finite; a program needn't handle non-finite values.
Results may differ from the reference program's by a relative error of at most 0.012.
The reference program's roundings to bfloat16 on the way (of `normed`, `queries`, `keys`, `values`, `weights` and `attended`) count: a program that leaves them out, or rounds other values in their place, can miss the bound.
Values may be sent and summed in bfloat16 or wider, within the bound.
A program may use at most 64 MiB of HBM per device.

```python
import jax
import jax.numpy as jnp
from jax import lax

D = 4608
QH = 16
KVH = 8
HD = 128
WIN = 4096
TOK_DEV = 512
TOKENS = 2048
N_SEQ = 4


def projection_pair(key):
    base_key, noise_key = jax.random.split(jax.random.fold_in(key, 7), 2)
    base = jax.random.normal(base_key, (D, QH * HD), jnp.float32) / jnp.sqrt(float(D))
    noise = jax.random.normal(noise_key, (D, KVH * HD), jnp.float32) / jnp.sqrt(float(D))
    query_part = base
    key_part = noise
    return (jnp.clip(query_part, -1.0, 1.0), jnp.clip(key_part, -1.0, 1.0))


def draw_query_weight(key, part):
    return projection_pair(key)[0].astype(jnp.bfloat16)


def draw_key_weight(key, part):
    return projection_pair(key)[1].astype(jnp.bfloat16)


def draw_tokens(key, part):
    main_key = jax.random.fold_in(jax.random.fold_in(key, 11), 0)
    raw = jax.random.normal(main_key, (TOKENS, D), jnp.float32)
    return jnp.clip(raw, -14.0, 14.0).astype(jnp.bfloat16)


def draw_positions(key, part):
    border_key = jax.random.fold_in(key, 3)
    border = jax.random.randint(border_key, (), TOKENS // 4, 3 * TOKENS // 4 + 1)
    offset = TOKENS - border
    index = jnp.arange(TOKENS, dtype=jnp.int32)
    return jnp.where(index < border, offset + index, index - border).astype(jnp.int32)


def level_of(stream_key, shape, cuts, least, top_value):
    gain = 1.0
    for dim, blocks in cuts:
        draws = jax.random.uniform(jax.random.fold_in(jax.random.fold_in(stream_key, 6), dim), (blocks,), jnp.float32, least / len(cuts), top_value / len(cuts))
        gain = gain * jnp.repeat(jnp.exp(draws), shape[dim] // blocks).reshape((-1,) + (1,) * (len(shape) - 1 - dim))
    return gain


def scatter_about(rng, shape, scale, most, cuts=(), held_as=jnp.bfloat16):
    result = scale * jax.random.normal(rng, shape, jnp.float32)
    if cuts:
        result = result * level_of(rng, shape, cuts, -0.22, 0.18)
    return jnp.clip(result, -most, most).astype(held_as)


def setup_inputs(seed: int = 0, part: int = 0) -> dict:
    splits = jax.random.split(jax.random.key(seed), 8)
    part_keys = jax.random.split(jax.random.fold_in(splits[7], part), 8)
    tokens = draw_tokens(jax.random.fold_in(jax.random.fold_in(splits[7], part), 71), part)
    norm_gain = jnp.clip(jax.random.uniform(splits[1], (D,), jnp.float32, 0.5, 1.5), 0.5, 1.5)
    query_weight = draw_query_weight(jax.random.fold_in(splits[7], 71), part)
    key_weight = draw_key_weight(jax.random.fold_in(splits[7], 71), part)
    value_weight = scatter_about(splits[4], (D, KVH * HD), D ** -0.5, 0.09375, ((0, 4), (1, 4)))
    out_weight = scatter_about(splits[5], (QH * HD, D), (QH * HD // 64) ** -0.5, 1.0, ((0, 4), (1, 4)))
    positions = draw_positions(jax.random.fold_in(jax.random.fold_in(splits[7], part), 71), part)
    return dict(tokens=tokens, norm_gain=norm_gain, query_weight=query_weight, key_weight=key_weight, value_weight=value_weight, out_weight=out_weight, positions=positions)


score_scale = 1.0 / 12.0
rope_base = 10000.0

def rms_norm(values_in, norm_gain):
    floats = values_in.astype(jnp.float32)
    square_mean = lax.optimization_barrier(jnp.mean(floats * floats, axis=-1, keepdims=True))
    return (floats * lax.rsqrt(square_mean + 1e-06) * norm_gain.astype(jnp.float32)).astype(jnp.bfloat16)

def rotate(heads_in, places):
    width = heads_in.shape[-1]
    half = width // 2
    inverse = jnp.exp(-jnp.log(rope_base) * jnp.arange(half, dtype=jnp.float32) * (2.0 / width))
    angle = places.astype(jnp.float32)[:, None] * inverse[None, :]
    cosine = jnp.cos(angle)[:, None, :]
    sine = jnp.sin(angle)[:, None, :]
    lower = heads_in[..., :half]
    upper = heads_in[..., half:]
    return jnp.concatenate([lower * cosine - upper * sine, upper * cosine + lower * sine], axis=-1)

def reference(tokens, norm_gain, query_weight, key_weight, value_weight, out_weight, positions):
    normed = rms_norm(tokens, norm_gain)
    queries = rotate(jnp.dot(normed, query_weight, preferred_element_type=jnp.float32).reshape(TOKENS, QH, HD), positions).astype(jnp.bfloat16)
    keys = rotate(jnp.dot(normed, key_weight, preferred_element_type=jnp.float32).reshape(TOKENS, KVH, HD), positions).astype(jnp.bfloat16)
    values = jnp.dot(normed, value_weight, preferred_element_type=jnp.float32).astype(jnp.bfloat16).reshape(TOKENS, KVH, HD)
    reach = WIN // TOK_DEV
    lead = reach * TOK_DEV
    keys_pad = jnp.concatenate([jnp.zeros((lead, KVH, HD), jnp.bfloat16), keys], axis=0)
    values_pad = jnp.concatenate([jnp.zeros((lead, KVH, HD), jnp.bfloat16), values], axis=0)
    places_pad = jnp.concatenate([jnp.zeros((lead,), jnp.int32), positions.astype(jnp.int32)], axis=0)
    span = (reach + 1) * TOK_DEV

    def one_shard(shard):
        start = (shard * TOK_DEV).astype(jnp.int32)
        query_block = lax.dynamic_slice_in_dim(queries, start, TOK_DEV, 0)
        key_block = lax.dynamic_slice_in_dim(keys_pad, start, span, 0)
        value_block = lax.dynamic_slice_in_dim(values_pad, start, span, 0)
        query_places = lax.dynamic_slice_in_dim(positions.astype(jnp.int32), start, TOK_DEV, 0)
        key_places = lax.dynamic_slice_in_dim(places_pad, start, span, 0)
        query_index = start + jnp.arange(TOK_DEV, dtype=jnp.int32)
        key_index = start - lead + jnp.arange(span, dtype=jnp.int32)
        distance = query_index[:, None] - key_index[None, :]
        visible = (key_index[None, :] >= 0) & (distance >= 0) & (distance < WIN)
        visible = visible & (query_places[:, None] - key_places[None, :] == distance)
        grouped = query_block.reshape(TOK_DEV, KVH, 2, HD).astype(jnp.float32)
        scores = jnp.einsum('qgeh,kgh->qgek', grouped, key_block.astype(jnp.float32)) * score_scale
        scores = jnp.where(visible[:, None, None, :], scores, -1e+30)
        largest = lax.optimization_barrier(jnp.max(scores, axis=-1, keepdims=True))
        weights = jnp.exp(scores - largest)
        total = lax.optimization_barrier(jnp.sum(weights, axis=-1))
        rounded = lax.optimization_barrier(weights.astype(jnp.bfloat16)).astype(jnp.float32)
        summed = jnp.einsum('qgek,kgh->qgeh', rounded, value_block.astype(jnp.float32))
        return (summed / total[..., None]).astype(jnp.bfloat16).reshape(TOK_DEV, QH * HD)
    attended = lax.map(one_shard, jnp.arange(N_SEQ, dtype=jnp.int32)).reshape(TOKENS, QH * HD)
    projected = jnp.dot(attended, out_weight, preferred_element_type=jnp.float32)
    return (tokens.astype(jnp.float32) + projected).astype(jnp.bfloat16)
```

```python
import jax
import jax.numpy as jnp
from jax import lax
from jax.experimental import pallas as pl
from jax.experimental.pallas import tpu as pltpu
from jax.sharding import PartitionSpec as P

KVH = 8
HD = 128
WIN = 4096


score_scale = 1.0 / 12.0
rope_base = 10000.0


def passed_along(block, axis, distance):
    devices = range(lax.axis_size(axis))
    route = [(i - distance, i) for i in devices if i - distance in devices]
    return lax.ppermute(block, axis, route)


def rms_norm(values_in, norm_gain):
    floats = values_in.astype(jnp.float32)
    square_mean = jnp.mean(floats * floats, axis=-1, keepdims=True)
    return (floats * lax.rsqrt(square_mean + 1e-06) * norm_gain).astype(jnp.bfloat16)


def rotate(heads_in, places):
    width = heads_in.shape[-1]
    half = width // 2
    inverse = jnp.exp(-jnp.log(rope_base) * jnp.arange(half, dtype=jnp.float32) * (2.0 / width))
    angle = places.astype(jnp.float32)[:, None] * inverse[None, :]
    cosine = jnp.cos(angle)[:, None, :]
    sine = jnp.sin(angle)[:, None, :]
    lower = heads_in[..., :half]
    upper = heads_in[..., half:]
    return jnp.concatenate([lower * cosine - upper * sine, upper * cosine + lower * sine], axis=-1)


def per_device(tokens, norm_gain, query_weight, key_weight, value_weight, out_weight, positions):
    tok_rows = tokens.shape[0]
    col_count = lax.axis_size("col")
    seq_count = lax.axis_size("seq")
    seq_index = lax.axis_index("seq")
    kv_local = KVH // col_count
    whole = lax.all_gather(tokens, "col", axis=1, tiled=True)
    normed = rms_norm(whole, norm_gain)
    all_places = lax.all_gather(positions, "seq", axis=0, tiled=True)
    pieces = (
        lax.all_gather(query_weight, "seq", axis=0, tiled=True),
        lax.all_gather(key_weight, "seq", axis=0, tiled=True),
        lax.all_gather(value_weight, "seq", axis=0, tiled=True),
    )
    columns = normed
    query_raw, key_raw, value_raw = tuple(
        (jnp.dot(columns, piece, preferred_element_type=jnp.float32) for piece in pieces)
    )
    queries = (
        rotate(query_raw.reshape(tok_rows, 2 * kv_local, HD), positions)
        .astype(jnp.bfloat16)
        .reshape(tok_rows, kv_local, 2, HD)
    )
    keys = (
        rotate(key_raw.reshape(tok_rows, kv_local, HD), positions)
        .astype(jnp.bfloat16)
        .reshape(tok_rows, kv_local * HD)
    )
    values = value_raw.astype(jnp.bfloat16)
    packed = jnp.stack([keys, values])
    reach = min(WIN // tok_rows, seq_count - 1)
    blocks = [packed]
    current = packed
    for step in range(reach):
        current = passed_along(current, "seq", 1)
        blocks.insert(0, current)
    window = jnp.concatenate(blocks, axis=1)
    span = (reach + 1) * tok_rows
    places_pad = jnp.concatenate([jnp.zeros((reach * tok_rows,), jnp.int32), all_places], axis=0)
    key_places = lax.dynamic_slice_in_dim(places_pad, seq_index * tok_rows, span, 0)
    key_index = (seq_index - reach) * tok_rows + jnp.arange(span, dtype=jnp.int32)
    query_index = seq_index * tok_rows + jnp.arange(tok_rows, dtype=jnp.int32)
    group = 1
    for candidate in range(1, reach + 2):
        if (reach + 1) % candidate == 0 and candidate * tok_rows <= max(512, tok_rows):
            group = candidate
    key_rows = group * tok_rows
    key_blocks = span // key_rows
    keys_blocked = window[0].reshape(key_blocks, key_rows, kv_local, HD)[::-1]
    values_blocked = window[1].reshape(key_blocks, key_rows, kv_local, HD)[::-1]
    places_blocked = key_places.reshape(key_blocks, key_rows)[::-1]
    index_blocked = key_index.reshape(key_blocks, key_rows)[::-1]

    def attend(carry, block):
        largest, total, summed = carry
        key_part, value_part, place_part, index_part = block
        scores = (
            jnp.einsum("qgeh,kgh->qgek", queries, key_part, preferred_element_type=jnp.float32)
            * score_scale
        )
        distance = query_index[:, None] - index_part[None, :]
        visible = (index_part[None, :] >= 0) & (distance >= 0) & (distance < WIN)
        visible = visible & (positions[:, None] - place_part[None, :] == distance)
        scores = jnp.where(visible[:, None, None, :], scores, -1e30)
        newest = jnp.maximum(largest, jnp.max(scores, axis=-1))
        factor = jnp.exp(largest - newest)
        weights = jnp.exp(scores - newest[..., None])
        total = total * factor + jnp.sum(weights, axis=-1)
        summed = summed * factor[..., None] + jnp.einsum(
            "qgek,kgh->qgeh",
            weights.astype(jnp.bfloat16),
            value_part,
            preferred_element_type=jnp.float32,
        )
        return ((newest, total, summed), None)

    start_state = (
        jnp.full((tok_rows, kv_local, 2), -1e30, jnp.float32),
        jnp.zeros((tok_rows, kv_local, 2), jnp.float32),
        jnp.zeros((tok_rows, kv_local, 2, HD), jnp.float32),
    )
    final_state, unused = lax.scan(
        attend, start_state, (keys_blocked, values_blocked, places_blocked, index_blocked)
    )
    attended = (
        (final_state[2] / final_state[1][..., None])
        .astype(jnp.bfloat16)
        .reshape(tok_rows, 2 * kv_local * HD)
    )
    mixed = lax.all_gather(attended, "col", axis=1, tiled=True)
    columns = mixed
    projected = jnp.dot(
        columns,
        lax.all_gather(out_weight, "seq", axis=0, tiled=True),
        preferred_element_type=jnp.float32,
    )
    return (tokens.astype(jnp.float32) + projected).astype(jnp.bfloat16)


MESH = pl.DeviceIdType.MESH
N_SEQ = 4
N_COL = 4
LOG2E = 1.4426950408889634
KEY, VAL, QUE, OUT = range(4)


def block_kernel(
    tok, gain, kw, vw, qw, ow, cosine, sine, first,
    out,
    x_all, normed, wk, wv, wq, wo, keys, values, queries, mixed,
    z_send, z_recv, y_send, y_recv, t_send, t_recv, l_sem, k_send, k_recv, a_send, a_recv,
):
    g = lax.axis_index("grp")
    s = lax.axis_index("seq")
    c = lax.axis_index("col")
    sources = (kw, vw, qw, ow)
    gathered = (wk, wv, wq, wo)
    signs = (1, -1)
    rows = tok.shape[0]
    feats = tok.shape[1]
    kv_cols = kw.shape[1]
    kv_local = kv_cols // HD

    def half(a, which):
        size = sources[a].shape[0] // 2
        return pl.ds(pl.multiple_of(which * size, 16), size)

    def came(d, r):
        return (s - r >= 0) if d == 0 else (s + r < N_SEQ)

    def has_next(d):
        return (s + 1 < N_SEQ) if d == 0 else (s >= 1)

    def z_copy(a, d, r):
        b = s - signs[d] * (r - 1)
        mine = half(a, g)
        src = sources[a].at[mine] if r == 1 else gathered[a].at[b, mine]
        return pltpu.make_async_remote_copy(
            src, gathered[a].at[b, mine], z_send.at[a, d, r - 1], z_recv.at[a, d, r - 1],
            device_id={"seq": s + signs[d]}, device_id_type=MESH)

    def z_wait(a, d, r):
        ref = gathered[a].at[s - signs[d] * r, half(a, g)]
        pltpu.make_async_remote_copy(
            ref, ref, z_send.at[a, d, r - 1], z_recv.at[a, d, r - 1],
            device_id={"seq": s - signs[d]}, device_id_type=MESH).wait_recv()

    def y_copy(a, d, r, which):
        ref = gathered[a].at[s - signs[d] * r, half(a, which)]
        return pltpu.make_async_remote_copy(
            ref, ref, y_send.at[a, d, r - 1], y_recv.at[a, d, r - 1],
            device_id={"grp": 1 - g}, device_id_type=MESH)

    def begin(names):
        for d in range(2):
            @pl.when(has_next(d))
            def _():
                for a in names:
                    z_copy(a, d, 1).start()

    def pass_on(names, r):
        for d in range(2):
            @pl.when(came(d, r))
            def _():
                for a in names:
                    z_wait(a, d, r)
                    if r < N_SEQ - 1:
                        @pl.when(has_next(d))
                        def _():
                            z_copy(a, d, r + 1).start()
                    y_copy(a, d, r, g).start()

    def arrived(names):
        for a in names:
            for d in range(2):
                for r in range(1, N_SEQ):
                    @pl.when(came(d, r))
                    def _():
                        y_copy(a, d, r, 1 - g).wait_recv()

    def col_copy(src, dst_of, sender, k, send, recv):
        return pltpu.make_async_remote_copy(
            src, dst_of(sender), send, recv,
            device_id={"col": lax.rem(c + k, N_COL)}, device_id_type=MESH)

    def token_copy(k, sender):
        return col_copy(tok, lambda i: x_all.at[i], sender, k, t_send.at[k - 1], t_recv.at[k - 1])

    def mixed_copy(k, e, sender):
        part = lambda i: mixed.at[i, :, pl.ds(e * 2 * HD, 2 * HD)]
        return col_copy(part(c), part, sender, k, a_send.at[k - 1, e], a_recv.at[k - 1, e])

    def kv_copy(which, d):
        ref = (keys, values)[which]
        return pltpu.make_async_remote_copy(
            ref.at[0], ref.at[d], k_send.at[which, d - 1], k_recv.at[which, d - 1],
            device_id={"seq": s + d}, device_id_type=MESH)

    barrier = pltpu.get_barrier_semaphore()
    pl.semaphore_signal(barrier, inc=1, device_id={"grp": 1 - g}, device_id_type=MESH)
    for k in range(1, N_COL):
        pl.semaphore_signal(
            barrier, inc=1, device_id={"col": lax.rem(c + k, N_COL)}, device_id_type=MESH)
    for d in (-2, -1, 1, 2):
        @pl.when((s + d >= 0) & (s + d < N_SEQ))
        def _():
            pl.semaphore_signal(barrier, inc=1, device_id={"seq": s + d}, device_id_type=MESH)
    inner = jnp.where((s >= 1) & (s < N_SEQ - 1), 1, 0)
    pl.semaphore_wait(barrier, N_COL + 2 + inner)

    begin((KEY, VAL))
    for k in range(1, N_COL):
        token_copy(k, c).start()
    local = [pltpu.make_async_copy(tok, x_all.at[c], l_sem.at[4])]
    for a in (KEY, VAL, QUE, OUT):
        local.append(pltpu.make_async_copy(sources[a], gathered[a].at[s], l_sem.at[a]))
    for copy in local:
        copy.start()

    for d in (1, 2):
        @pl.when(s < d)
        def _():
            keys[d] = jnp.zeros_like(keys[d])
            values[d] = jnp.zeros_like(values[d])

    pass_on((KEY, VAL), 1)
    begin((QUE,))
    pass_on((KEY, VAL), 2)
    pass_on((QUE,), 1)
    begin((OUT,))
    pass_on((KEY, VAL), 3)

    for copy in local:
        copy.wait()
    for k in range(1, N_COL):
        token_copy(k, lax.rem(c + N_COL - k, N_COL)).wait_recv()

    step = 64

    def norm_rows(t, carry):
        at = pl.ds(pl.multiple_of(t * step, step), step)
        total = jnp.zeros((step, 1), jnp.float32)
        for b in range(N_COL):
            f = x_all[b, at, :].astype(jnp.float32)
            total = total + jnp.sum(f * f, axis=-1, keepdims=True)
        scale = lax.rsqrt(total / (N_COL * feats) + 1e-06)
        for b in range(N_COL):
            f = x_all[b, at, :].astype(jnp.float32)
            normed[b, at, :] = (f * scale * gain[b]).astype(jnp.bfloat16)
        return carry

    lax.fori_loop(0, rows // step, norm_rows, 0)
    pass_on((QUE,), 2)
    arrived((KEY, VAL))

    tile = 256

    def project(at, weight, lo):
        total = jnp.dot(normed[0, at, :], weight[0, :, lo:lo + 256],
                        preferred_element_type=jnp.float32)
        for b in range(1, N_SEQ):
            total = total + jnp.dot(normed[b, at, :], weight[b, :, lo:lo + 256],
                                    preferred_element_type=jnp.float32)
        return total

    def turned(raw, at):
        parts = []
        for h in range(raw.shape[1] // HD):
            u = raw[:, h * HD:(h + 1) * HD]
            swapped = jnp.concatenate([u[:, HD // 2:], u[:, :HD // 2]], axis=1)
            parts.append(u * cosine[at, :] + swapped * sine[at, :])
        return jnp.concatenate(parts, axis=1).astype(jnp.bfloat16)

    def kv_rows(t, carry):
        at = pl.ds(pl.multiple_of(t * tile, tile), tile)
        keys[0, at, :] = turned(project(at, wk, 0), at)
        values[0, at, :] = project(at, wv, 0).astype(jnp.bfloat16)
        return carry

    lax.fori_loop(0, rows // tile, kv_rows, 0)
    for d in (1, 2):
        @pl.when(s + d < N_SEQ)
        def _():
            for which in range(2):
                kv_copy(which, d).start()

    pass_on((OUT,), 1)
    pass_on((QUE,), 3)
    arrived((QUE,))

    def q_rows(t, carry):
        at = pl.ds(pl.multiple_of(t * tile, tile), tile)
        for lo in range(0, qw.shape[1], 256):
            queries[at, lo:lo + 256] = turned(project(at, wq, lo), at)
        return carry

    lax.fori_loop(0, rows // tile, q_rows, 0)
    pass_on((OUT,), 2)
    for d in (1, 2):
        @pl.when(s >= d)
        def _():
            for which in range(2):
                ref = (keys, values)[which].at[d]
                pltpu.make_async_remote_copy(
                    ref, ref, k_send.at[which, d - 1], k_recv.at[which, d - 1],
                    device_id={"seq": s - d}, device_id_type=MESH).wait_recv()

    q_tile = 128

    def attend_rows(e):
        def body(t, carry):
            at = pl.ds(pl.multiple_of(t * q_tile, q_tile), q_tile)
            here = s * rows + t * q_tile + lax.broadcasted_iota(jnp.int32, (q_tile, rows), 0)
            earliest = jnp.maximum(first[at, :], 0)
            shown = []
            for d in range(3):
                there = (s - d) * rows + lax.broadcasted_iota(jnp.int32, (q_tile, rows), 1)
                ok = there >= earliest
                if d == 0:
                    ok = ok & (there <= here)
                shown.append(ok)
            lanes = slice(e * HD, (e + 1) * HD)
            for h in range(2):
                q_lanes = slice((2 * e + h) * HD, (2 * e + h + 1) * HD)
                q = queries[at, q_lanes]
                scores = []
                for d in range(3):
                    raw = lax.dot_general(
                        q, keys[d, :, lanes], (((1,), (1,)), ((), ())),
                        preferred_element_type=jnp.float32) * (score_scale * LOG2E)
                    scores.append(jnp.where(shown[d], raw, -1e30))
                top = jnp.maximum(jnp.maximum(scores[0], scores[1]), scores[2])
                largest = jnp.max(top, axis=-1, keepdims=True)
                total = jnp.zeros((q_tile, rows), jnp.float32)
                summed = jnp.zeros((q_tile, HD), jnp.float32)
                for d in range(3):
                    w = jnp.exp2(scores[d] - largest)
                    total = total + w
                    summed = summed + jnp.dot(
                        w.astype(jnp.bfloat16), values[d, :, lanes],
                        preferred_element_type=jnp.float32)
                total = jnp.sum(total, axis=-1, keepdims=True)
                mixed[c, at, q_lanes] = (summed / total).astype(jnp.bfloat16)
            return carry

        lax.fori_loop(0, rows // q_tile, body, 0)

    for e in range(kv_local):
        attend_rows(e)
        for k in range(1, N_COL):
            mixed_copy(k, e, c).start()
        if e == 0:
            pass_on((OUT,), 3)

    arrived((OUT,))
    for k in range(1, N_COL):
        for e in range(kv_local):
            mixed_copy(k, e, lax.rem(c + N_COL - k, N_COL)).wait_recv()

    def out_rows(t, carry):
        at = pl.ds(pl.multiple_of(t * tile, tile), tile)
        for lo in range(0, feats, 384):
            cols = slice(lo, lo + 384)
            total = jnp.dot(mixed[0, at, :], wo[0, :, cols], preferred_element_type=jnp.float32)
            for b in range(1, N_COL):
                total = total + jnp.dot(
                    mixed[b, at, :], wo[b, :, cols], preferred_element_type=jnp.float32)
            out[at, cols] = (x_all[c, at, cols].astype(jnp.float32) + total).astype(jnp.bfloat16)
        return carry

    lax.fori_loop(0, rows // tile, out_rows, 0)

    for a in range(4):
        for d in range(2):
            for r in range(1, N_SEQ):
                @pl.when(came(d, r - 1) & has_next(d))
                def _():
                    z_copy(a, d, r).wait_send()

                @pl.when(came(d, r))
                def _():
                    y_copy(a, d, r, g).wait_send()
    for k in range(1, N_COL):
        token_copy(k, c).wait_send()
        for e in range(kv_local):
            mixed_copy(k, e, c).wait_send()
    for d in (1, 2):
        @pl.when(s + d < N_SEQ)
        def _():
            for which in range(2):
                kv_copy(which, d).wait_send()


def fused_device(tokens, norm_gain, query_weight, key_weight, value_weight, out_weight, positions):
    rows, feats = tokens.shape
    half = HD // 2
    inverse = jnp.exp(-jnp.log(rope_base) * jnp.arange(half, dtype=jnp.float32) * (2.0 / HD))
    angle = positions.astype(jnp.float32)[:, None] * inverse[None, :]
    cosine = jnp.cos(angle)
    sine = jnp.sin(angle)
    cosine = jnp.concatenate([cosine, cosine], axis=1)
    sine = jnp.concatenate([-sine, sine], axis=1)
    index = lax.axis_index("seq") * rows + jnp.arange(rows, dtype=jnp.int32)
    first = (index - positions)[:, None]
    gain = norm_gain.reshape(N_COL, 1, feats)
    bf16 = jnp.bfloat16
    dma = pltpu.SemaphoreType.DMA
    anywhere = pl.BlockSpec(memory_space=pl.ANY)
    vmem = pl.BlockSpec(memory_space=pltpu.VMEM)
    kv_cols = key_weight.shape[1]
    q_cols = query_weight.shape[1]
    return pl.pallas_call(
        block_kernel,
        out_shape=jax.ShapeDtypeStruct((rows, feats), bf16),
        in_specs=[anywhere, vmem, anywhere, anywhere, anywhere, anywhere, vmem, vmem, vmem],
        out_specs=vmem,
        scratch_shapes=[
            pltpu.VMEM((N_COL, rows, feats), bf16),
            pltpu.VMEM((N_COL, rows, feats), bf16),
            pltpu.VMEM((N_SEQ,) + key_weight.shape, bf16),
            pltpu.VMEM((N_SEQ,) + value_weight.shape, bf16),
            pltpu.VMEM((N_SEQ,) + query_weight.shape, bf16),
            pltpu.VMEM((N_SEQ,) + out_weight.shape, bf16),
            pltpu.VMEM((3, rows, kv_cols), bf16),
            pltpu.VMEM((3, rows, kv_cols), bf16),
            pltpu.VMEM((rows, q_cols), bf16),
            pltpu.VMEM((N_COL, rows, q_cols), bf16),
            dma((4, 2, 3)), dma((4, 2, 3)), dma((4, 2, 3)), dma((4, 2, 3)),
            dma((3,)), dma((3,)), dma((5,)), dma((2, 2)), dma((2, 2)), dma((3, 2)), dma((3, 2)),
        ],
        compiler_params=pltpu.CompilerParams(
            collective_id=0, has_side_effects=True, vmem_limit_bytes=52 * 1024 * 1024),
    )(tokens, gain, key_weight, value_weight, query_weight, out_weight, cosine, sine, first)


def solution(mesh):
    small = (mesh.shape["grp"], mesh.shape["seq"], mesh.shape["col"]) == (2, N_SEQ, N_COL)
    return jax.shard_map(
        fused_device if small else per_device,
        mesh=mesh,
        in_specs=(
            P(("grp", "seq"), "col"),
            P(),
            P("seq", "col"),
            P("seq", "col"),
            P("seq", "col"),
            P("seq", "col"),
            P(("grp", "seq")),
        ),
        out_specs=P(("grp", "seq"), "col"),
        check_vma=False,
    )
```

```python
import jax
import jax.numpy as jnp
from jax import lax
from jax.experimental import pallas as pl
from jax.experimental.pallas import tpu as pltpu
from jax.sharding import PartitionSpec as P

KVH = 8
HD = 128
WIN = 4096


score_scale = 1.0 / 12.0
rope_base = 10000.0


def passed_along(block, axis, distance):
    devices = range(lax.axis_size(axis))
    route = [(i - distance, i) for i in devices if i - distance in devices]
    return lax.ppermute(block, axis, route)


def rms_norm(values_in, norm_gain):
    floats = values_in.astype(jnp.float32)
    square_mean = jnp.mean(floats * floats, axis=-1, keepdims=True)
    return (floats * lax.rsqrt(square_mean + 1e-06) * norm_gain).astype(jnp.bfloat16)


def rotate(heads_in, places):
    width = heads_in.shape[-1]
    half = width // 2
    inverse = jnp.exp(-jnp.log(rope_base) * jnp.arange(half, dtype=jnp.float32) * (2.0 / width))
    angle = places.astype(jnp.float32)[:, None] * inverse[None, :]
    cosine = jnp.cos(angle)[:, None, :]
    sine = jnp.sin(angle)[:, None, :]
    lower = heads_in[..., :half]
    upper = heads_in[..., half:]
    return jnp.concatenate([lower * cosine - upper * sine, upper * cosine + lower * sine], axis=-1)


def per_device(tokens, norm_gain, query_weight, key_weight, value_weight, out_weight, positions):
    tok_rows = tokens.shape[0]
    col_count = lax.axis_size("col")
    seq_count = lax.axis_size("seq")
    seq_index = lax.axis_index("seq")
    kv_local = KVH // col_count
    whole = lax.all_gather(tokens, "col", axis=1, tiled=True)
    normed = rms_norm(whole, norm_gain)
    all_places = lax.all_gather(positions, "seq", axis=0, tiled=True)
    pieces = (
        lax.all_gather(query_weight, "seq", axis=0, tiled=True),
        lax.all_gather(key_weight, "seq", axis=0, tiled=True),
        lax.all_gather(value_weight, "seq", axis=0, tiled=True),
    )
    columns = normed
    query_raw, key_raw, value_raw = tuple(
        (jnp.dot(columns, piece, preferred_element_type=jnp.float32) for piece in pieces)
    )
    queries = (
        rotate(query_raw.reshape(tok_rows, 2 * kv_local, HD), positions)
        .astype(jnp.bfloat16)
        .reshape(tok_rows, kv_local, 2, HD)
    )
    keys = (
        rotate(key_raw.reshape(tok_rows, kv_local, HD), positions)
        .astype(jnp.bfloat16)
        .reshape(tok_rows, kv_local * HD)
    )
    values = value_raw.astype(jnp.bfloat16)
    packed = jnp.stack([keys, values])
    reach = min(WIN // tok_rows, seq_count - 1)
    blocks = [packed]
    current = packed
    for step in range(reach):
        current = passed_along(current, "seq", 1)
        blocks.insert(0, current)
    window = jnp.concatenate(blocks, axis=1)
    span = (reach + 1) * tok_rows
    places_pad = jnp.concatenate([jnp.zeros((reach * tok_rows,), jnp.int32), all_places], axis=0)
    key_places = lax.dynamic_slice_in_dim(places_pad, seq_index * tok_rows, span, 0)
    key_index = (seq_index - reach) * tok_rows + jnp.arange(span, dtype=jnp.int32)
    query_index = seq_index * tok_rows + jnp.arange(tok_rows, dtype=jnp.int32)
    group = 1
    for candidate in range(1, reach + 2):
        if (reach + 1) % candidate == 0 and candidate * tok_rows <= max(512, tok_rows):
            group = candidate
    key_rows = group * tok_rows
    key_blocks = span // key_rows
    keys_blocked = window[0].reshape(key_blocks, key_rows, kv_local, HD)[::-1]
    values_blocked = window[1].reshape(key_blocks, key_rows, kv_local, HD)[::-1]
    places_blocked = key_places.reshape(key_blocks, key_rows)[::-1]
    index_blocked = key_index.reshape(key_blocks, key_rows)[::-1]

    def attend(carry, block):
        largest, total, summed = carry
        key_part, value_part, place_part, index_part = block
        scores = (
            jnp.einsum("qgeh,kgh->qgek", queries, key_part, preferred_element_type=jnp.float32)
            * score_scale
        )
        distance = query_index[:, None] - index_part[None, :]
        visible = (index_part[None, :] >= 0) & (distance >= 0) & (distance < WIN)
        visible = visible & (positions[:, None] - place_part[None, :] == distance)
        scores = jnp.where(visible[:, None, None, :], scores, -1e30)
        newest = jnp.maximum(largest, jnp.max(scores, axis=-1))
        factor = jnp.exp(largest - newest)
        weights = jnp.exp(scores - newest[..., None])
        total = total * factor + jnp.sum(weights, axis=-1)
        summed = summed * factor[..., None] + jnp.einsum(
            "qgek,kgh->qgeh",
            weights.astype(jnp.bfloat16),
            value_part,
            preferred_element_type=jnp.float32,
        )
        return ((newest, total, summed), None)

    start_state = (
        jnp.full((tok_rows, kv_local, 2), -1e30, jnp.float32),
        jnp.zeros((tok_rows, kv_local, 2), jnp.float32),
        jnp.zeros((tok_rows, kv_local, 2, HD), jnp.float32),
    )
    final_state, unused = lax.scan(
        attend, start_state, (keys_blocked, values_blocked, places_blocked, index_blocked)
    )
    attended = (
        (final_state[2] / final_state[1][..., None])
        .astype(jnp.bfloat16)
        .reshape(tok_rows, 2 * kv_local * HD)
    )
    mixed = lax.all_gather(attended, "col", axis=1, tiled=True)
    columns = mixed
    projected = jnp.dot(
        columns,
        lax.all_gather(out_weight, "seq", axis=0, tiled=True),
        preferred_element_type=jnp.float32,
    )
    return (tokens.astype(jnp.float32) + projected).astype(jnp.bfloat16)


MESH = pl.DeviceIdType.MESH
N_SEQ = 4
N_COL = 4
LOG2E = 1.4426950408889634
KEY, VAL, QUE, OUT = range(4)
PIECES = ((KEY, 0, 1), (VAL, 0, 1), (QUE, 0, 2), (QUE, 1, 2), (OUT, 0, 2), (OUT, 1, 2))
K_0, V_0, Q_0, Q_1, O_0, O_1 = range(6)


def block_kernel(
    tok, gain, kw, vw, qw, ow, cosine, sine, first,
    out,
    x_all, normed, wk, wv, wq, wo, keys, values, queries, mixed,
    z_send, z_recv, y_send, y_recv, t_send, t_recv, l_sem, k_send, k_recv, a_send, a_recv,
):
    g = lax.axis_index("grp")
    s = lax.axis_index("seq")
    c = lax.axis_index("col")
    sources = (kw, vw, qw, ow)
    gathered = (wk, wv, wq, wo)
    signs = (1, -1)
    rows = tok.shape[0]
    feats = tok.shape[1]
    kv_cols = kw.shape[1]
    kv_local = kv_cols // HD

    def half(p, which):
        a, part, parts = PIECES[p]
        size = sources[a].shape[0] // (2 * parts)
        return pl.ds(pl.multiple_of((which * parts + part) * size, 16), size)

    def place(p, b, which):
        return gathered[PIECES[p][0]].at[b, half(p, which)]

    def came(d, r):
        return (s - r >= 0) if d == 0 else (s + r < N_SEQ)

    def has_next(d):
        return (s + 1 < N_SEQ) if d == 0 else (s >= 1)

    def z_copy(p, d, r):
        b = s - signs[d] * (r - 1)
        ref = place(p, b, g)
        src = sources[PIECES[p][0]].at[half(p, g)] if r == 1 else ref
        return pltpu.make_async_remote_copy(
            src, ref, z_send.at[p, d, r - 1], z_recv.at[p, d, r - 1],
            device_id={"seq": s + signs[d]}, device_id_type=MESH)

    def z_wait(p, d, r):
        ref = place(p, s - signs[d] * r, g)
        pltpu.make_async_remote_copy(
            ref, ref, z_send.at[p, d, r - 1], z_recv.at[p, d, r - 1],
            device_id={"seq": s - signs[d]}, device_id_type=MESH).wait_recv()

    def y_copy(p, d, r, which):
        ref = place(p, s - signs[d] * r, which)
        return pltpu.make_async_remote_copy(
            ref, ref, y_send.at[p, d, r - 1], y_recv.at[p, d, r - 1],
            device_id={"grp": 1 - g}, device_id_type=MESH)

    def begin(names):
        for d in range(2):
            @pl.when(has_next(d))
            def _():
                for a in names:
                    z_copy(a, d, 1).start()

    def pass_on(names, r):
        for d in range(2):
            @pl.when(came(d, r))
            def _():
                for a in names:
                    z_wait(a, d, r)
                    if r < N_SEQ - 1:
                        @pl.when(has_next(d))
                        def _():
                            z_copy(a, d, r + 1).start()
                    y_copy(a, d, r, g).start()

    def arrived(names):
        for a in names:
            for d in range(2):
                for r in range(1, N_SEQ):
                    @pl.when(came(d, r))
                    def _():
                        y_copy(a, d, r, 1 - g).wait_recv()

    core = c + 1 - 2 * lax.rem(c, 2)
    across = lax.rem(c + 2, N_COL)
    far = lax.rem(core + 2, N_COL)

    def token_copy(k, block):
        src = x_all.at[block] if k == 2 else tok
        return pltpu.make_async_remote_copy(
            src, x_all.at[block], t_send.at[k], t_recv.at[k],
            device_id={"col": across if k == 0 else core}, device_id_type=MESH)

    def mixed_copy(k, e, block):
        ref = mixed.at[block, :, pl.ds(e * 2 * HD, 2 * HD)]
        return pltpu.make_async_remote_copy(
            ref, ref, a_send.at[k, e], a_recv.at[k, e],
            device_id={"col": across if k == 0 else core}, device_id_type=MESH)

    def mixed_on(e):
        mixed_copy(0, e, across).wait_recv()
        mixed_copy(2, e, across).start()

    def kv_copy(which, d):
        ref = (keys, values)[which]
        return pltpu.make_async_remote_copy(
            ref.at[0], ref.at[d], k_send.at[which, d - 1], k_recv.at[which, d - 1],
            device_id={"seq": s + d}, device_id_type=MESH)

    barrier = pltpu.get_barrier_semaphore()
    pl.semaphore_signal(barrier, inc=1, device_id={"grp": 1 - g}, device_id_type=MESH)
    for k in range(1, N_COL):
        pl.semaphore_signal(
            barrier, inc=1, device_id={"col": lax.rem(c + k, N_COL)}, device_id_type=MESH)
    for d in (-2, -1, 1, 2):
        @pl.when((s + d >= 0) & (s + d < N_SEQ))
        def _():
            pl.semaphore_signal(barrier, inc=1, device_id={"seq": s + d}, device_id_type=MESH)
    inner = jnp.where((s >= 1) & (s < N_SEQ - 1), 1, 0)
    pl.semaphore_wait(barrier, N_COL + 2 + inner)

    begin((K_0, V_0))
    for k in range(2):
        token_copy(k, c).start()
    local = [pltpu.make_async_copy(tok, x_all.at[c], l_sem.at[4])]
    for a in (KEY, VAL, QUE, OUT):
        local.append(pltpu.make_async_copy(sources[a], gathered[a].at[s], l_sem.at[a]))
    for copy in local:
        copy.start()

    for d in (1, 2):
        @pl.when(s < d)
        def _():
            keys[d] = jnp.zeros_like(keys[d])
            values[d] = jnp.zeros_like(values[d])

    pass_on((K_0, V_0), 1)
    begin((Q_0,))
    pass_on((K_0, V_0), 2)
    token_copy(0, across).wait_recv()
    token_copy(2, across).start()
    begin((Q_1,))
    pass_on((Q_0,), 1)
    pass_on((K_0, V_0), 3)
    pass_on((Q_1,), 1)

    for copy in local:
        copy.wait()
    token_copy(1, core).wait_recv()
    token_copy(2, far).wait_recv()

    step = 64

    def norm_rows(t, carry):
        at = pl.ds(pl.multiple_of(t * step, step), step)
        total = jnp.zeros((step, 1), jnp.float32)
        for b in range(N_COL):
            f = x_all[b, at, :].astype(jnp.float32)
            total = total + jnp.sum(f * f, axis=-1, keepdims=True)
        scale = lax.rsqrt(total / (N_COL * feats) + 1e-06)
        for b in range(N_COL):
            f = x_all[b, at, :].astype(jnp.float32)
            normed[b, at, :] = (f * scale * gain[b]).astype(jnp.bfloat16)
        return carry

    lax.fori_loop(0, rows // step, norm_rows, 0)
    pass_on((Q_0,), 2)
    arrived((K_0, V_0))

    tile = 256

    def project(at, weight, lo):
        total = jnp.dot(normed[0, at, :], weight[0, :, lo:lo + 256],
                        preferred_element_type=jnp.float32)
        for b in range(1, N_SEQ):
            total = total + jnp.dot(normed[b, at, :], weight[b, :, lo:lo + 256],
                                    preferred_element_type=jnp.float32)
        return total

    def turned(raw, at):
        parts = []
        for h in range(raw.shape[1] // HD):
            u = raw[:, h * HD:(h + 1) * HD]
            swapped = jnp.concatenate([u[:, HD // 2:], u[:, :HD // 2]], axis=1)
            parts.append(u * cosine[at, :] + swapped * sine[at, :])
        return jnp.concatenate(parts, axis=1).astype(jnp.bfloat16)

    def kv_rows(t, carry):
        at = pl.ds(pl.multiple_of(t * tile, tile), tile)
        keys[0, at, :] = turned(project(at, wk, 0), at)
        values[0, at, :] = project(at, wv, 0).astype(jnp.bfloat16)
        return carry

    lax.fori_loop(0, rows // tile, kv_rows, 0)
    for d in (1, 2):
        @pl.when(s + d < N_SEQ)
        def _():
            for which in range(2):
                kv_copy(which, d).start()

    pass_on((Q_1,), 2)
    begin((O_0,))
    pass_on((Q_0,), 3)
    begin((O_1,))
    pass_on((Q_1,), 3)
    pass_on((O_0,), 1)
    arrived((Q_0, Q_1))

    def q_rows(t, carry):
        at = pl.ds(pl.multiple_of(t * tile, tile), tile)
        for lo in range(0, qw.shape[1], 256):
            queries[at, lo:lo + 256] = turned(project(at, wq, lo), at)
        return carry

    lax.fori_loop(0, rows // tile, q_rows, 0)
    pass_on((O_1,), 1)
    for d in (1, 2):
        @pl.when(s >= d)
        def _():
            for which in range(2):
                ref = (keys, values)[which].at[d]
                pltpu.make_async_remote_copy(
                    ref, ref, k_send.at[which, d - 1], k_recv.at[which, d - 1],
                    device_id={"seq": s - d}, device_id_type=MESH).wait_recv()

    q_tile = 128

    def attend_rows(e, lo, hi):
        def body(t, carry):
            at = pl.ds(pl.multiple_of(t * q_tile, q_tile), q_tile)
            here = s * rows + t * q_tile + lax.broadcasted_iota(jnp.int32, (q_tile, rows), 0)
            earliest = jnp.maximum(first[at, :], 0)
            shown = []
            for d in range(3):
                there = (s - d) * rows + lax.broadcasted_iota(jnp.int32, (q_tile, rows), 1)
                ok = there >= earliest
                if d == 0:
                    ok = ok & (there <= here)
                shown.append(ok)
            lanes = slice(e * HD, (e + 1) * HD)
            for h in range(2):
                q_lanes = slice((2 * e + h) * HD, (2 * e + h + 1) * HD)
                q = queries[at, q_lanes]
                scores = []
                for d in range(3):
                    raw = lax.dot_general(
                        q, keys[d, :, lanes], (((1,), (1,)), ((), ())),
                        preferred_element_type=jnp.float32) * (score_scale * LOG2E)
                    scores.append(jnp.where(shown[d], raw, -1e30))
                top = jnp.maximum(jnp.maximum(scores[0], scores[1]), scores[2])
                largest = jnp.max(top, axis=-1, keepdims=True)
                total = jnp.zeros((q_tile, rows), jnp.float32)
                summed = jnp.zeros((q_tile, HD), jnp.float32)
                for d in range(3):
                    w = jnp.exp2(scores[d] - largest)
                    total = total + w
                    summed = summed + jnp.dot(
                        w.astype(jnp.bfloat16), values[d, :, lanes],
                        preferred_element_type=jnp.float32)
                total = jnp.sum(total, axis=-1, keepdims=True)
                mixed[c, at, q_lanes] = (summed / total).astype(jnp.bfloat16)
            return carry

        lax.fori_loop(lo, hi, body, 0)

    tiles = rows // q_tile

    def share(e):
        for k in range(2):
            mixed_copy(k, e, c).start()

    attend_rows(0, 0, tiles)
    share(0)
    pass_on((O_0,), 2)
    attend_rows(1, 0, tiles // 2)
    pass_on((O_1,), 2)
    attend_rows(1, tiles // 2, tiles)
    share(1)
    mixed_on(0)
    mixed_on(1)
    pass_on((O_0,), 3)
    pass_on((O_1,), 3)

    for e in range(kv_local):
        mixed_copy(1, e, core).wait_recv()
        mixed_copy(2, e, far).wait_recv()
    arrived((O_0, O_1))

    def out_rows(t, carry):
        at = pl.ds(pl.multiple_of(t * tile, tile), tile)
        for lo in range(0, feats, 384):
            cols = slice(lo, lo + 384)
            total = jnp.dot(mixed[0, at, :], wo[0, :, cols], preferred_element_type=jnp.float32)
            for b in range(1, N_COL):
                total = total + jnp.dot(
                    mixed[b, at, :], wo[b, :, cols], preferred_element_type=jnp.float32)
            out[at, cols] = (x_all[c, at, cols].astype(jnp.float32) + total).astype(jnp.bfloat16)
        return carry

    lax.fori_loop(0, rows // tile, out_rows, 0)

    for a in range(len(PIECES)):
        for d in range(2):
            for r in range(1, N_SEQ):
                @pl.when(came(d, r - 1) & has_next(d))
                def _():
                    z_copy(a, d, r).wait_send()

                @pl.when(came(d, r))
                def _():
                    y_copy(a, d, r, g).wait_send()
    for k in range(N_COL - 1):
        token_copy(k, across if k == 2 else c).wait_send()
        for e in range(kv_local):
            mixed_copy(k, e, across if k == 2 else c).wait_send()
    for d in (1, 2):
        @pl.when(s + d < N_SEQ)
        def _():
            for which in range(2):
                kv_copy(which, d).wait_send()


def fused_device(tokens, norm_gain, query_weight, key_weight, value_weight, out_weight, positions):
    rows, feats = tokens.shape
    half = HD // 2
    inverse = jnp.exp(-jnp.log(rope_base) * jnp.arange(half, dtype=jnp.float32) * (2.0 / HD))
    angle = positions.astype(jnp.float32)[:, None] * inverse[None, :]
    cosine = jnp.cos(angle)
    sine = jnp.sin(angle)
    cosine = jnp.concatenate([cosine, cosine], axis=1)
    sine = jnp.concatenate([-sine, sine], axis=1)
    index = lax.axis_index("seq") * rows + jnp.arange(rows, dtype=jnp.int32)
    first = (index - positions)[:, None]
    gain = norm_gain.reshape(N_COL, 1, feats)
    bf16 = jnp.bfloat16
    dma = pltpu.SemaphoreType.DMA
    anywhere = pl.BlockSpec(memory_space=pl.ANY)
    vmem = pl.BlockSpec(memory_space=pltpu.VMEM)
    kv_cols = key_weight.shape[1]
    q_cols = query_weight.shape[1]
    return pl.pallas_call(
        block_kernel,
        out_shape=jax.ShapeDtypeStruct((rows, feats), bf16),
        in_specs=[anywhere, vmem, anywhere, anywhere, anywhere, anywhere, vmem, vmem, vmem],
        out_specs=vmem,
        scratch_shapes=[
            pltpu.VMEM((N_COL, rows, feats), bf16),
            pltpu.VMEM((N_COL, rows, feats), bf16),
            pltpu.VMEM((N_SEQ,) + key_weight.shape, bf16),
            pltpu.VMEM((N_SEQ,) + value_weight.shape, bf16),
            pltpu.VMEM((N_SEQ,) + query_weight.shape, bf16),
            pltpu.VMEM((N_SEQ,) + out_weight.shape, bf16),
            pltpu.VMEM((3, rows, kv_cols), bf16),
            pltpu.VMEM((3, rows, kv_cols), bf16),
            pltpu.VMEM((rows, q_cols), bf16),
            pltpu.VMEM((N_COL, rows, q_cols), bf16),
            dma((6, 2, 3)), dma((6, 2, 3)), dma((6, 2, 3)), dma((6, 2, 3)),
            dma((3,)), dma((3,)), dma((5,)), dma((2, 2)), dma((2, 2)), dma((3, 2)), dma((3, 2)),
        ],
        compiler_params=pltpu.CompilerParams(
            collective_id=0, has_side_effects=True, vmem_limit_bytes=52 * 1024 * 1024),
    )(tokens, gain, key_weight, value_weight, query_weight, out_weight, cosine, sine, first)


def solution(mesh):
    small = (mesh.shape["grp"], mesh.shape["seq"], mesh.shape["col"]) == (2, N_SEQ, N_COL)
    return jax.shard_map(
        fused_device if small else per_device,
        mesh=mesh,
        in_specs=(
            P(("grp", "seq"), "col"),
            P(),
            P("seq", "col"),
            P("seq", "col"),
            P("seq", "col"),
            P("seq", "col"),
            P(("grp", "seq")),
        ),
        out_specs=P(("grp", "seq"), "col"),
        check_vma=False,
    )
```

```python
import jax
import jax.numpy as jnp
from jax import lax
from jax.experimental import pallas as pl
from jax.experimental.pallas import tpu as pltpu
from jax.sharding import PartitionSpec as P

KVH = 8
HD = 128
WIN = 4096


score_scale = 1.0 / 12.0
rope_base = 10000.0


def passed_along(block, axis, distance):
    devices = range(lax.axis_size(axis))
    route = [(i - distance, i) for i in devices if i - distance in devices]
    return lax.ppermute(block, axis, route)


def rms_norm(values_in, norm_gain):
    floats = values_in.astype(jnp.float32)
    square_mean = jnp.mean(floats * floats, axis=-1, keepdims=True)
    return (floats * lax.rsqrt(square_mean + 1e-06) * norm_gain).astype(jnp.bfloat16)


def rotate(heads_in, places):
    width = heads_in.shape[-1]
    half = width // 2
    inverse = jnp.exp(-jnp.log(rope_base) * jnp.arange(half, dtype=jnp.float32) * (2.0 / width))
    angle = places.astype(jnp.float32)[:, None] * inverse[None, :]
    cosine = jnp.cos(angle)[:, None, :]
    sine = jnp.sin(angle)[:, None, :]
    lower = heads_in[..., :half]
    upper = heads_in[..., half:]
    return jnp.concatenate([lower * cosine - upper * sine, upper * cosine + lower * sine], axis=-1)


def per_device(tokens, norm_gain, query_weight, key_weight, value_weight, out_weight, positions):
    tok_rows = tokens.shape[0]
    col_count = lax.axis_size("col")
    seq_count = lax.axis_size("seq")
    seq_index = lax.axis_index("seq")
    kv_local = KVH // col_count
    whole = lax.all_gather(tokens, "col", axis=1, tiled=True)
    normed = rms_norm(whole, norm_gain)
    all_places = lax.all_gather(positions, "seq", axis=0, tiled=True)
    pieces = (
        lax.all_gather(query_weight, "seq", axis=0, tiled=True),
        lax.all_gather(key_weight, "seq", axis=0, tiled=True),
        lax.all_gather(value_weight, "seq", axis=0, tiled=True),
    )
    columns = normed
    query_raw, key_raw, value_raw = tuple(
        (jnp.dot(columns, piece, preferred_element_type=jnp.float32) for piece in pieces)
    )
    queries = (
        rotate(query_raw.reshape(tok_rows, 2 * kv_local, HD), positions)
        .astype(jnp.bfloat16)
        .reshape(tok_rows, kv_local, 2, HD)
    )
    keys = (
        rotate(key_raw.reshape(tok_rows, kv_local, HD), positions)
        .astype(jnp.bfloat16)
        .reshape(tok_rows, kv_local * HD)
    )
    values = value_raw.astype(jnp.bfloat16)
    packed = jnp.stack([keys, values])
    reach = min(WIN // tok_rows, seq_count - 1)
    blocks = [packed]
    current = packed
    for step in range(reach):
        current = passed_along(current, "seq", 1)
        blocks.insert(0, current)
    window = jnp.concatenate(blocks, axis=1)
    span = (reach + 1) * tok_rows
    places_pad = jnp.concatenate([jnp.zeros((reach * tok_rows,), jnp.int32), all_places], axis=0)
    key_places = lax.dynamic_slice_in_dim(places_pad, seq_index * tok_rows, span, 0)
    key_index = (seq_index - reach) * tok_rows + jnp.arange(span, dtype=jnp.int32)
    query_index = seq_index * tok_rows + jnp.arange(tok_rows, dtype=jnp.int32)
    group = 1
    for candidate in range(1, reach + 2):
        if (reach + 1) % candidate == 0 and candidate * tok_rows <= max(512, tok_rows):
            group = candidate
    key_rows = group * tok_rows
    key_blocks = span // key_rows
    keys_blocked = window[0].reshape(key_blocks, key_rows, kv_local, HD)[::-1]
    values_blocked = window[1].reshape(key_blocks, key_rows, kv_local, HD)[::-1]
    places_blocked = key_places.reshape(key_blocks, key_rows)[::-1]
    index_blocked = key_index.reshape(key_blocks, key_rows)[::-1]

    def attend(carry, block):
        largest, total, summed = carry
        key_part, value_part, place_part, index_part = block
        scores = (
            jnp.einsum("qgeh,kgh->qgek", queries, key_part, preferred_element_type=jnp.float32)
            * score_scale
        )
        distance = query_index[:, None] - index_part[None, :]
        visible = (index_part[None, :] >= 0) & (distance >= 0) & (distance < WIN)
        visible = visible & (positions[:, None] - place_part[None, :] == distance)
        scores = jnp.where(visible[:, None, None, :], scores, -1e30)
        newest = jnp.maximum(largest, jnp.max(scores, axis=-1))
        factor = jnp.exp(largest - newest)
        weights = jnp.exp(scores - newest[..., None])
        total = total * factor + jnp.sum(weights, axis=-1)
        summed = summed * factor[..., None] + jnp.einsum(
            "qgek,kgh->qgeh",
            weights.astype(jnp.bfloat16),
            value_part,
            preferred_element_type=jnp.float32,
        )
        return ((newest, total, summed), None)

    start_state = (
        jnp.full((tok_rows, kv_local, 2), -1e30, jnp.float32),
        jnp.zeros((tok_rows, kv_local, 2), jnp.float32),
        jnp.zeros((tok_rows, kv_local, 2, HD), jnp.float32),
    )
    final_state, unused = lax.scan(
        attend, start_state, (keys_blocked, values_blocked, places_blocked, index_blocked)
    )
    attended = (
        (final_state[2] / final_state[1][..., None])
        .astype(jnp.bfloat16)
        .reshape(tok_rows, 2 * kv_local * HD)
    )
    mixed = lax.all_gather(attended, "col", axis=1, tiled=True)
    columns = mixed
    projected = jnp.dot(
        columns,
        lax.all_gather(out_weight, "seq", axis=0, tiled=True),
        preferred_element_type=jnp.float32,
    )
    return (tokens.astype(jnp.float32) + projected).astype(jnp.bfloat16)


MESH = pl.DeviceIdType.MESH
N_SEQ = 4
N_COL = 4
LOG2E = 1.4426950408889634
KEY, VAL, QUE, OUT = range(4)
PIECES = ((KEY, 0, 1), (VAL, 0, 1), (QUE, 0, 2), (QUE, 1, 2), (OUT, 0, 4), (OUT, 1, 4), (OUT, 2, 4), (OUT, 3, 4))
K_0, V_0, Q_0, Q_1, O_0, O_1, O_2, O_3 = range(8)


def block_kernel(
    tok, gain, kw, vw, qw, ow, cosine, sine, first,
    out,
    x_all, normed, wk, wv, wq, wo, keys, values, queries, mixed, total,
    z_send, z_recv, y_send, y_recv, t_send, t_recv, l_sem, k_send, k_recv, a_send, a_recv,
):
    g = lax.axis_index("grp")
    s = lax.axis_index("seq")
    c = lax.axis_index("col")
    sources = (kw, vw, qw, ow)
    gathered = (wk, wv, wq, wo)
    signs = (1, -1)
    rows = tok.shape[0]
    feats = tok.shape[1]
    kv_cols = kw.shape[1]
    kv_local = kv_cols // HD

    def half(p, which):
        a, part, parts = PIECES[p]
        size = sources[a].shape[0] // (2 * parts)
        return pl.ds(pl.multiple_of((which * parts + part) * size, 16), size)

    def place(p, b, which):
        return gathered[PIECES[p][0]].at[b, half(p, which)]

    def came(d, r):
        return (s - r >= 0) if d == 0 else (s + r < N_SEQ)

    def has_next(d):
        return (s + 1 < N_SEQ) if d == 0 else (s >= 1)

    def z_copy(p, d, r):
        b = s - signs[d] * (r - 1)
        ref = place(p, b, g)
        src = sources[PIECES[p][0]].at[half(p, g)] if r == 1 else ref
        return pltpu.make_async_remote_copy(
            src, ref, z_send.at[p, d, r - 1], z_recv.at[p, d, r - 1],
            device_id={"seq": s + signs[d]}, device_id_type=MESH)

    def z_wait(p, d, r):
        ref = place(p, s - signs[d] * r, g)
        pltpu.make_async_remote_copy(
            ref, ref, z_send.at[p, d, r - 1], z_recv.at[p, d, r - 1],
            device_id={"seq": s - signs[d]}, device_id_type=MESH).wait_recv()

    def y_copy(p, d, r, which):
        ref = place(p, s - signs[d] * r, which)
        return pltpu.make_async_remote_copy(
            ref, ref, y_send.at[p, d, r - 1], y_recv.at[p, d, r - 1],
            device_id={"grp": 1 - g}, device_id_type=MESH)

    def begin(names):
        for d in range(2):
            @pl.when(has_next(d))
            def _():
                for a in names:
                    z_copy(a, d, 1).start()

    def pass_on(names, r):
        for d in range(2):
            @pl.when(came(d, r))
            def _():
                for a in names:
                    z_wait(a, d, r)
                    if r < N_SEQ - 1:
                        @pl.when(has_next(d))
                        def _():
                            z_copy(a, d, r + 1).start()
                    y_copy(a, d, r, g).start()

    def arrived(names):
        for a in names:
            for d in range(2):
                for r in range(1, N_SEQ):
                    @pl.when(came(d, r))
                    def _():
                        y_copy(a, d, r, 1 - g).wait_recv()

    core = c + 1 - 2 * lax.rem(c, 2)
    across = lax.rem(c + 2, N_COL)
    far = lax.rem(core + 2, N_COL)

    def token_copy(k, block):
        src = x_all.at[block] if k == 2 else tok
        return pltpu.make_async_remote_copy(
            src, x_all.at[block], t_send.at[k], t_recv.at[k],
            device_id={"col": across if k == 0 else core}, device_id_type=MESH)

    def mixed_copy(k, e, block):
        ref = mixed.at[block, :, pl.ds(e * 2 * HD, 2 * HD)]
        return pltpu.make_async_remote_copy(
            ref, ref, a_send.at[k, e], a_recv.at[k, e],
            device_id={"col": across if k == 0 else core}, device_id_type=MESH)

    def mixed_on(e):
        mixed_copy(0, e, across).wait_recv()
        mixed_copy(2, e, across).start()

    def kv_copy(which, d):
        ref = (keys, values)[which]
        return pltpu.make_async_remote_copy(
            ref.at[0], ref.at[d], k_send.at[which, d - 1], k_recv.at[which, d - 1],
            device_id={"seq": s + d}, device_id_type=MESH)

    barrier = pltpu.get_barrier_semaphore()
    pl.semaphore_signal(barrier, inc=1, device_id={"grp": 1 - g}, device_id_type=MESH)
    for k in range(1, N_COL):
        pl.semaphore_signal(
            barrier, inc=1, device_id={"col": lax.rem(c + k, N_COL)}, device_id_type=MESH)
    for d in (-2, -1, 1, 2):
        @pl.when((s + d >= 0) & (s + d < N_SEQ))
        def _():
            pl.semaphore_signal(barrier, inc=1, device_id={"seq": s + d}, device_id_type=MESH)
    inner = jnp.where((s >= 1) & (s < N_SEQ - 1), 1, 0)
    pl.semaphore_wait(barrier, N_COL + 2 + inner)

    begin((K_0, V_0))
    for k in range(2):
        token_copy(k, c).start()
    local = [pltpu.make_async_copy(tok, x_all.at[c], l_sem.at[4])]
    for a in (KEY, VAL, QUE, OUT):
        local.append(pltpu.make_async_copy(sources[a], gathered[a].at[s], l_sem.at[a]))
    for copy in local:
        copy.start()

    for d in (1, 2):
        @pl.when(s < d)
        def _():
            keys[d] = jnp.zeros_like(keys[d])
            values[d] = jnp.zeros_like(values[d])

    pass_on((K_0, V_0), 1)
    begin((Q_0,))
    pass_on((K_0, V_0), 2)
    token_copy(0, across).wait_recv()
    token_copy(2, across).start()
    begin((Q_1,))
    pass_on((Q_0,), 1)
    pass_on((K_0, V_0), 3)
    pass_on((Q_1,), 1)

    for copy in local:
        copy.wait()
    token_copy(1, core).wait_recv()
    token_copy(2, far).wait_recv()

    step = 64

    def norm_rows(t, carry):
        at = pl.ds(pl.multiple_of(t * step, step), step)
        total = jnp.zeros((step, 1), jnp.float32)
        for b in range(N_COL):
            f = x_all[b, at, :].astype(jnp.float32)
            total = total + jnp.sum(f * f, axis=-1, keepdims=True)
        scale = lax.rsqrt(total / (N_COL * feats) + 1e-06)
        for b in range(N_COL):
            f = x_all[b, at, :].astype(jnp.float32)
            normed[b, at, :] = (f * scale * gain[b * feats:(b + 1) * feats]).astype(jnp.bfloat16)
        return carry

    lax.fori_loop(0, rows // step, norm_rows, 0)
    pass_on((Q_0,), 2)
    arrived((K_0, V_0))

    tile = 256

    def project(at, weight, lo):
        total = jnp.dot(normed[0, at, :], weight[0, :, lo:lo + 256],
                        preferred_element_type=jnp.float32)
        for b in range(1, N_SEQ):
            total = total + jnp.dot(normed[b, at, :], weight[b, :, lo:lo + 256],
                                    preferred_element_type=jnp.float32)
        return total

    def turned(raw, at):
        parts = []
        for h in range(raw.shape[1] // HD):
            u = raw[:, h * HD:(h + 1) * HD]
            swapped = jnp.concatenate([u[:, HD // 2:], u[:, :HD // 2]], axis=1)
            parts.append(u * cosine[at, :] + swapped * sine[at, :])
        return jnp.concatenate(parts, axis=1).astype(jnp.bfloat16)

    def kv_rows(t, carry):
        at = pl.ds(pl.multiple_of(t * tile, tile), tile)
        keys[0, at, :] = turned(project(at, wk, 0), at)
        values[0, at, :] = project(at, wv, 0).astype(jnp.bfloat16)
        return carry

    lax.fori_loop(0, rows // tile, kv_rows, 0)
    for d in (1, 2):
        @pl.when(s + d < N_SEQ)
        def _():
            for which in range(2):
                kv_copy(which, d).start()

    pass_on((Q_1,), 2)
    begin((O_0, O_1))
    pass_on((Q_0,), 3)
    begin((O_2, O_3))
    pass_on((Q_1,), 3)
    pass_on((O_0, O_1), 1)
    arrived((Q_0, Q_1))

    def q_rows(t, carry):
        at = pl.ds(pl.multiple_of(t * tile, tile), tile)
        for lo in range(0, qw.shape[1], 256):
            queries[at, lo:lo + 256] = turned(project(at, wq, lo), at)
        return carry

    lax.fori_loop(0, rows // tile, q_rows, 0)
    pass_on((O_2, O_3), 1)
    for d in (1, 2):
        @pl.when(s >= d)
        def _():
            for which in range(2):
                ref = (keys, values)[which].at[d]
                pltpu.make_async_remote_copy(
                    ref, ref, k_send.at[which, d - 1], k_recv.at[which, d - 1],
                    device_id={"seq": s - d}, device_id_type=MESH).wait_recv()

    q_tile = 128

    def attend_rows(e, lo, hi):
        def body(t, carry):
            at = pl.ds(pl.multiple_of(t * q_tile, q_tile), q_tile)
            here = s * rows + t * q_tile + lax.broadcasted_iota(jnp.int32, (q_tile, rows), 0)
            earliest = jnp.maximum(first[at, :], 0)
            shown = []
            for d in range(3):
                there = (s - d) * rows + lax.broadcasted_iota(jnp.int32, (q_tile, rows), 1)
                ok = there >= earliest
                if d == 0:
                    ok = ok & (there <= here)
                shown.append(ok)
            lanes = slice(e * HD, (e + 1) * HD)
            for h in range(2):
                q_lanes = slice((2 * e + h) * HD, (2 * e + h + 1) * HD)
                q = queries[at, q_lanes]
                scores = []
                for d in range(3):
                    raw = lax.dot_general(
                        q, keys[d, :, lanes], (((1,), (1,)), ((), ())),
                        preferred_element_type=jnp.float32) * (score_scale * LOG2E)
                    scores.append(jnp.where(shown[d], raw, -1e30))
                top = jnp.maximum(jnp.maximum(scores[0], scores[1]), scores[2])
                largest = jnp.max(top, axis=-1, keepdims=True)
                total = jnp.zeros((q_tile, rows), jnp.float32)
                summed = jnp.zeros((q_tile, HD), jnp.float32)
                for d in range(3):
                    w = jnp.exp2(scores[d] - largest)
                    total = total + w
                    summed = summed + jnp.dot(
                        w.astype(jnp.bfloat16), values[d, :, lanes],
                        preferred_element_type=jnp.float32)
                total = jnp.sum(total, axis=-1, keepdims=True)
                mixed[c, at, q_lanes] = (summed / total).astype(jnp.bfloat16)
            return carry

        lax.fori_loop(lo, hi, body, 0)

    tiles = rows // q_tile

    def share(e):
        for k in range(2):
            mixed_copy(k, e, c).start()

    attend_rows(0, 0, tiles)
    share(0)
    pass_on((O_0, O_1), 2)
    attend_rows(1, 0, tiles // 2)
    pass_on((O_2, O_3), 2)
    attend_rows(1, tiles // 2, tiles)
    share(1)
    mixed_on(0)
    mixed_on(1)
    for e in range(kv_local):
        mixed_copy(1, e, core).wait_recv()
        mixed_copy(2, e, far).wait_recv()
    width = 384

    def add_rows(b):
        def body(t, carry):
            at = pl.ds(pl.multiple_of(t * tile, tile), tile)
            for lo in range(0, feats, width):
                cols = slice(lo, lo + width)
                total[at, cols] = total[at, cols] + jnp.dot(
                    mixed[b, at, :], wo[b, :, cols], preferred_element_type=jnp.float32)
            return carry

        lax.fori_loop(0, rows // tile, body, 0)

    def start_rows(t, carry):
        at = pl.ds(pl.multiple_of(t * tile, tile), tile)
        for lo in range(0, feats, width):
            cols = slice(lo, lo + width)
            total[at, cols] = x_all[c, at, cols].astype(jnp.float32) + jnp.dot(
                mixed[s, at, :], wo[s, :, cols], preferred_element_type=jnp.float32)
        return carry

    lax.fori_loop(0, rows // tile, start_rows, 0)
    o_all = (O_0, O_1, O_2, O_3)
    for r in range(1, N_SEQ):
        if r == N_SEQ - 1:
            for p in o_all:
                pass_on((p,), r)
        for d in range(2):
            @pl.when(came(d, r))
            def _():
                for p in o_all:
                    y_copy(p, d, r, 1 - g).wait_recv()
                add_rows(s - signs[d] * r)

    def out_rows(t, carry):
        at = pl.ds(pl.multiple_of(t * tile, tile), tile)
        out[at, :] = total[at, :].astype(jnp.bfloat16)
        return carry

    lax.fori_loop(0, rows // tile, out_rows, 0)

    for a in range(len(PIECES)):
        for d in range(2):
            for r in range(1, N_SEQ):
                @pl.when(came(d, r - 1) & has_next(d))
                def _():
                    z_copy(a, d, r).wait_send()

                @pl.when(came(d, r))
                def _():
                    y_copy(a, d, r, g).wait_send()
    for k in range(N_COL - 1):
        token_copy(k, across if k == 2 else c).wait_send()
        for e in range(kv_local):
            mixed_copy(k, e, across if k == 2 else c).wait_send()
    for d in (1, 2):
        @pl.when(s + d < N_SEQ)
        def _():
            for which in range(2):
                kv_copy(which, d).wait_send()


def fused_device(tokens, norm_gain, query_weight, key_weight, value_weight, out_weight, positions):
    rows, feats = tokens.shape
    half = HD // 2
    inverse = jnp.exp(-jnp.log(rope_base) * jnp.arange(half, dtype=jnp.float32) * (2.0 / HD))
    angle = positions.astype(jnp.float32)[:, None] * inverse[None, :]
    cosine = jnp.cos(angle)
    sine = jnp.sin(angle)
    cosine = jnp.concatenate([cosine, cosine], axis=1)
    sine = jnp.concatenate([-sine, sine], axis=1)
    index = lax.axis_index("seq") * rows + jnp.arange(rows, dtype=jnp.int32)
    first = (index - positions)[:, None]
    bf16 = jnp.bfloat16
    dma = pltpu.SemaphoreType.DMA
    anywhere = pl.BlockSpec(memory_space=pl.ANY)
    vmem = pl.BlockSpec(memory_space=pltpu.VMEM)
    kv_cols = key_weight.shape[1]
    q_cols = query_weight.shape[1]
    return pl.pallas_call(
        block_kernel,
        out_shape=jax.ShapeDtypeStruct((rows, feats), bf16),
        in_specs=[anywhere, vmem, anywhere, anywhere, anywhere, anywhere, vmem, vmem, vmem],
        out_specs=vmem,
        scratch_shapes=[
            pltpu.VMEM((N_COL, rows, feats), bf16),
            pltpu.VMEM((N_COL, rows, feats), bf16),
            pltpu.VMEM((N_SEQ,) + key_weight.shape, bf16),
            pltpu.VMEM((N_SEQ,) + value_weight.shape, bf16),
            pltpu.VMEM((N_SEQ,) + query_weight.shape, bf16),
            pltpu.VMEM((N_SEQ,) + out_weight.shape, bf16),
            pltpu.VMEM((3, rows, kv_cols), bf16),
            pltpu.VMEM((3, rows, kv_cols), bf16),
            pltpu.VMEM((rows, q_cols), bf16),
            pltpu.VMEM((N_COL, rows, q_cols), bf16),
            pltpu.VMEM((rows, feats), jnp.float32),
            dma((8, 2, 3)), dma((8, 2, 3)), dma((8, 2, 3)), dma((8, 2, 3)),
            dma((3,)), dma((3,)), dma((5,)), dma((2, 2)), dma((2, 2)), dma((3, 2)), dma((3, 2)),
        ],
        compiler_params=pltpu.CompilerParams(
            collective_id=0, has_side_effects=True, vmem_limit_bytes=52 * 1024 * 1024),
    )(tokens, norm_gain, key_weight, value_weight, query_weight, out_weight, cosine, sine, first)


def solution(mesh):
    small = (mesh.shape["grp"], mesh.shape["seq"], mesh.shape["col"]) == (2, N_SEQ, N_COL)
    return jax.shard_map(
        fused_device if small else per_device,
        mesh=mesh,
        in_specs=(
            P(("grp", "seq"), "col"),
            P(),
            P("seq", "col"),
            P("seq", "col"),
            P("seq", "col"),
            P("seq", "col"),
            P(("grp", "seq")),
        ),
        out_specs=P(("grp", "seq"), "col"),
        check_vma=False,
    )
```
